256 devices in a mesh: dp: 8 (over x, z_hi), expert: 32 (over z_lo, y, core).
Axes of the slice: x: 4, y: 4, z: 8 (z_hi: 2, z_lo: 4; z = z_hi * 4 + z_lo), core: 2. Of those that a mesh axis runs over, the one named last changes fastest.
Arguments:
- moe_grad: bfloat16 [4096, 7168], P('expert', 'dp'), may hold values from -6 to 6
- saved_act: bfloat16 [4096, 8, 2, 1024], P('expert', None, None, 'dp'), may hold values from -6 to 6
- route_prob: bfloat16 [4096, 8], P('expert'), may hold values from 0.049804688 to 0.34960938
- expert_ids: int32 [4096, 8], P('expert'), may hold values from 0 to 31, all different within a row; in each aligned block of 128 rows (0 to 127, 128 to 255, ...) at most 42 rows name the same one
- w_gate: bfloat16 [32, 7168, 1024], P('expert', 'dp'), may hold values from -0.0625 to 0.0625
- w_up: bfloat16 [32, 7168, 1024], P('expert', 'dp'), may hold values from -0.0625 to 0.0625
- w_down: bfloat16 [32, 1024, 7168], P('expert', None, 'dp'), may hold values from -0.1875 to 0.1875
- queries: bfloat16 [4096, 12288], P('dp', 'expert'), may hold values from -300 to 300
- latent: bfloat16 [4096, 512], P('expert'), may hold values from -6 to 6
- rope_keys: bfloat16 [4096, 64], P('expert'), may hold values from -5 to 5
- w_ukv: bfloat16 [512, 16384], P(None, 'expert'), may hold values from -0.25 to 0.25
- latent_b: bfloat16 [4096, 512], P('dp'), may hold values from -6 to 6
- grad_kv_b: bfloat16 [4096, 16384], P('dp', 'expert'), may hold values from -0.119628906 to 0.119628906
Outputs:
- moe_input_grad: bfloat16 [4096, 7168], P('expert', 'dp')
- attn_out: bfloat16 [4096, 8192], P('dp', 'expert')
- ukv_grad: float32 [512, 16384], P('dp', 'expert')
The draws below stay inside these ranges and needn't reach their ends.
Inputs may be any that keep to these rules, and one draw needn't show every extreme that they name: `expert_ids`: each token names 8 different experts. In the 128 tokens of one device (aligned blocks) no expert is named more than 42 times; in every draw some expert is named exactly 42 times in some block, and every expert is named somewhere.
All inputs are finite; a program needn't handle non-finite values.
Results may differ from the reference program's by a relative error of at most 0.015.
Values may be sent and summed in bfloat16 or wider, within the bound.
No kernel may reach another device: no remote copies, remote signals or barrier semaphores. Data moves between devices by JAX's collectives and lax.ppermute only.
A program may use at most 128 MiB of HBM per device.

```python
import math
import jax
import jax.numpy as jnp
import numpy as np
from jax import lax

D = 7168
FF = 1024
TOPK = 8
TOK_DEV = 128
SEQ = 4096
HEADS = 64
HD = 128
ROPE = 64
LAT = 512
EXPERTS = 32
TOKENS = 4096
MOST = 42
QK = 192


def rope_table(key):
    return jnp.clip(jax.random.normal(jax.random.fold_in(key, 901), (SEQ, ROPE), jnp.float32), -4.0, 4.0)


def draw_rope_keys(key, part):
    base = rope_table(key)
    return base.astype(jnp.bfloat16)


def draw_queries(key, part):
    key = jax.random.fold_in(key, 5)
    first_key = jax.random.fold_in(key, 0)
    values = jnp.clip(jax.random.normal(first_key, (SEQ, HEADS, QK), jnp.float32), -5.0, 5.0)
    return values.reshape(SEQ, HEADS * QK).astype(jnp.bfloat16)


def strengthened(entries, key, source, target, parts, factor):
    owner, partner = [(jnp.arange(entries.shape[axis_at]) // (entries.shape[axis_at] // parts)).reshape([-1 if axis == axis_at else 1 for axis in range(entries.ndim)]) for axis_at in (source, target)]
    chosen = jax.random.permutation(key, parts)[partner]
    strong = (owner == chosen) | (owner == (partner + parts // 2) % parts)
    return jnp.where(strong, factor * entries, entries)


def steps_of(rng, dims, cuts, least, top_value):
    def one(axis_at, parts):
        draws = jax.random.uniform(jax.random.fold_in(jax.random.fold_in(rng, 6), axis_at), (parts,), jnp.float32, least / len(cuts), top_value / len(cuts))
        return jnp.repeat(jnp.exp(draws), dims[axis_at] // parts).reshape((-1,) + (1,) * (len(dims) - axis_at - 1))

    gain = one(*cuts[0])
    for cut in cuts[1:]:
        gain = gain * one(*cut)
    return gain


def deal_out(stream_key, own, number, rows, amount, top, limit, skew):
    order = jax.random.permutation(stream_key, amount)
    crowded, usual = load_shares(amount, rows * top, limit, skew, True), load_shares(amount, rows * top, limit, skew, False)
    places = jnp.arange(amount)

    def named(sizes, rotation):
        used = int((sizes > 0).sum())
        fixed = max(1, used // 4)
        shifted = fixed + (places - fixed + rotation * (used - fixed)) % max(1, amount - fixed)
        return jnp.zeros((amount,), jnp.int32).at[order[jnp.where(places < fixed, places, shifted)]].set(jnp.asarray(sizes, jnp.int32))

    sizes = jnp.where(number % 4 == 0, named(crowded, number // 4), named(usual, number - number // 4 - 1))
    mixed = jax.random.permutation(jax.random.fold_in(own, 3), amount)
    giver, receiver = mixed[0:amount // 2 * 2:2], mixed[1:amount // 2 * 2:2]
    margin = jnp.minimum(sizes[giver] - 1, limit - sizes[receiver]) // 2
    margin = jnp.where((giver == order[0]) | (receiver == order[0]) | (sizes[receiver] == 0), 0, jnp.maximum(margin, 0))
    shifted = jax.random.randint(jax.random.fold_in(own, 4), (amount // 2,), 0, 1 << 20) % (margin + 1)
    sizes = sizes.at[giver].add(-shifted).at[receiver].add(shifted)
    members = jnp.searchsorted(jnp.cumsum(sizes), jnp.arange(rows * top), side="right").astype(jnp.int32)
    table = members.reshape(top, rows).T
    table = table[jax.random.permutation(jax.random.fold_in(own, 1), rows)]
    rotation = jax.random.randint(jax.random.fold_in(own, 2), (rows, 1), 0, top)
    return jnp.take_along_axis(table, (jnp.arange(top)[None, :] + rotation) % top, axis=1)


def load_shares(amount, total, limit, lean, full):
    loads = [(1 << 20) // math.isqrt(grade ** lean) + 1 for grade in range(1, amount + 1)]
    largest = limit if full else min(limit, max(-(-total // amount), total * loads[0] // sum(loads)))
    least = 1 if total - largest >= amount - 1 else 0
    given, spare = [largest] + [least] * (amount - 1), total - largest - least * (amount - 1)
    while spare > 0:
        movable = [i for i in range(1, amount) if given[i] < largest] or [i for i in range(1, amount) if given[i] < limit]
        pool, left = sum([loads[i] for i in movable]), spare
        for i in movable:
            extra = min(limit - given[i], max(1, left * loads[i] // pool), spare)
            given[i] = given[i] + extra
            spare = spare - extra
    return np.array(given)


def centred(own_key, extent, deviation, reach, cuts=(), held_as=jnp.bfloat16):
    level = steps_of(own_key, extent, cuts, -0.22, 0.18) if cuts else 1.0
    result = jax.random.normal(own_key, extent, jnp.float32) * deviation * level
    return jnp.minimum(jnp.maximum(result, -reach), reach).astype(held_as)


def heavy_noise(stream_key, extent, width, most, shards, heavy, held_as=jnp.bfloat16):
    result = width * jax.random.normal(stream_key, extent, jnp.float32)
    if shards:
        result = result * steps_of(stream_key, extent, shards, -0.22, 0.18)
    return jnp.clip(strengthened(result, jax.random.fold_in(stream_key, 3), *heavy), -most, most).astype(held_as)


def setup_inputs(seed: int = 0) -> dict:
    splits = jax.random.split(jax.random.key(seed), 14)
    moe_grad = centred(splits[0], (TOKENS, D), 1.0, 6.0, ((0, 32), (1, 8)))
    saved_act = centred(splits[1], (TOKENS, TOPK, 2, FF), 1.0, 6.0, ((0, 32), (3, 8)))
    route_prob = jnp.clip(0.049804688 + 0.2998047 * jax.random.uniform(splits[2], (TOKENS, TOPK), jnp.float32) ** steps_of(splits[2], (TOKENS, TOPK), ((0, 32),), -0.2, 0.2), 0.049804688, 0.34960938).astype(jnp.bfloat16)
    expert_ids_keys = jax.random.split(jax.random.fold_in(splits[3], 1), TOKENS // TOK_DEV)
    expert_ids_turns = jax.random.permutation(jax.random.fold_in(splits[3], 3), TOKENS // TOK_DEV)
    expert_ids = jax.vmap(lambda own, number: deal_out(jax.random.fold_in(splits[3], 2), own, number, TOK_DEV, EXPERTS, TOPK, MOST, 2))(expert_ids_keys, expert_ids_turns).reshape((TOKENS, TOPK))
    w_gate = centred(splits[4], (EXPERTS, D, FF), D ** -0.5, 0.0625, ((0, 32), (1, 8)))
    w_up = centred(splits[5], (EXPERTS, D, FF), D ** -0.5, 0.0625, ((0, 32), (1, 8)))
    w_down = centred(splits[6], (EXPERTS, FF, D), FF ** -0.5, 0.1875, ((0, 32), (2, 8)))
    queries = draw_queries(jax.random.fold_in(splits[13], 71), 0)
    latent = centred(splits[8], (SEQ, LAT), 1.0, 6.0, ((0, 32),))
    rope_keys = draw_rope_keys(jax.random.fold_in(splits[13], 71), 0)
    w_ukv = centred(splits[10], (LAT, HEADS * 2 * HD), LAT ** -0.5, 0.25, ((1, 32),))
    latent_b = heavy_noise(splits[11], (SEQ, LAT), 1.0, 6.0, ((0, 8),), (0, 1, 8, 2.0))
    grad_kv_b = centred(splits[12], (SEQ, HEADS * 2 * HD), 0.02, 0.119628906, ((0, 8), (1, 32)))
    return {"moe_grad": moe_grad, "saved_act": saved_act, "route_prob": route_prob, "expert_ids": expert_ids, "w_gate": w_gate, "w_up": w_up, "w_down": w_down, "queries": queries, "latent": latent, "rope_keys": rope_keys, "w_ukv": w_ukv, "latent_b": latent_b, "grad_kv_b": grad_kv_b}


def reference(moe_grad, saved_act, route_prob, expert_ids, w_gate, w_up, w_down, queries, latent, rope_keys, w_ukv, latent_b, grad_kv_b):
    contract_last = (((1,), (1,)), ((), ()))
    assign_total = TOKENS * TOPK
    bound_rows = EXPERTS * MOST
    flat_ids = expert_ids.reshape(-1)
    pad_grad = jnp.concatenate([moe_grad, jnp.zeros((1, D), jnp.bfloat16)], axis=0)
    pad_prob = jnp.concatenate([route_prob.reshape(-1), jnp.zeros((1,), jnp.bfloat16)])
    pad_saved = jnp.concatenate([saved_act.reshape(assign_total, 2, FF), jnp.zeros((1, 2, FF), jnp.bfloat16)], axis=0)

    def one_expert(running, expert_index):
        (picked,) = jnp.nonzero(flat_ids == expert_index, size=bound_rows, fill_value=assign_total)
        picked = picked.astype(jnp.int32)
        token_rows = (picked // TOPK).astype(jnp.int32)
        grad_rows = pad_grad[token_rows]
        hidden_grad = lax.dot_general(grad_rows, w_down[expert_index], contract_last, preferred_element_type=jnp.float32)
        saved_rows = pad_saved[picked].astype(jnp.float32)
        gate_pre = saved_rows[:, 0]
        up_pre = saved_rows[:, 1]
        scaled = pad_prob[picked].astype(jnp.float32)[:, None] * hidden_grad
        sigmoid_gate = jax.nn.sigmoid(gate_pre)
        grad_gate = (scaled * up_pre * sigmoid_gate * (1.0 + gate_pre * (1.0 - sigmoid_gate))).astype(jnp.bfloat16)
        grad_up = (scaled * gate_pre * sigmoid_gate).astype(jnp.bfloat16)
        contribution = lax.dot_general(grad_gate, w_gate[expert_index], contract_last, preferred_element_type=jnp.float32)
        contribution = contribution + lax.dot_general(grad_up, w_up[expert_index], contract_last, preferred_element_type=jnp.float32)
        rounded = lax.optimization_barrier(contribution.astype(jnp.bfloat16))
        running = running.at[token_rows].add(rounded.astype(jnp.float32))
        return running, None

    initial = jnp.zeros((TOKENS + 1, D), jnp.float32)
    running, _ = lax.scan(one_expert, initial, jnp.arange(EXPERTS, dtype=jnp.int32))
    moe_input_grad = running[:TOKENS].astype(jnp.bfloat16)

    score_scale = QK ** -0.5
    kv_weights = w_ukv.reshape(LAT, HEADS, 2 * HD).transpose(1, 0, 2)
    head_queries = queries.reshape(SEQ, HEADS, QK).transpose(1, 0, 2)
    causal = jnp.arange(SEQ)[:, None] >= jnp.arange(SEQ)[None, :]
    rope_float = rope_keys.astype(jnp.float32)

    def one_head(head_pair):
        head_query, head_weight = head_pair
        projected = jnp.dot(latent, head_weight, preferred_element_type=jnp.float32).astype(jnp.bfloat16)
        projected = lax.optimization_barrier(projected)
        keys_nope = projected[:, :HD].astype(jnp.float32)
        values = projected[:, HD:]
        query_float = head_query.astype(jnp.float32)
        scores = jnp.dot(query_float[:, :HD], keys_nope.T, precision=lax.Precision.HIGHEST)
        scores = scores + jnp.dot(query_float[:, HD:], rope_float.T, precision=lax.Precision.HIGHEST)
        scores = jnp.where(causal, scores * score_scale, jnp.float32(-1e30))
        maxima = jnp.max(scores, axis=1, keepdims=True)
        expo = jnp.exp(scores - maxima)
        weights = (expo / jnp.sum(expo, axis=1, keepdims=True)).astype(jnp.bfloat16)
        return jnp.dot(weights, values, preferred_element_type=jnp.float32).astype(jnp.bfloat16)

    per_head = lax.map(one_head, (head_queries, kv_weights))
    attn_out = per_head.transpose(1, 0, 2).reshape(SEQ, HEADS * HD)

    ukv_grad = jnp.dot(latent_b.T, grad_kv_b, preferred_element_type=jnp.float32)
    return (moe_input_grad, attn_out, ukv_grad)
```

```python
import jax
import jax.numpy as jnp
from jax import lax
from jax.experimental import pallas as pl
from jax.experimental.pallas import tpu as pltpu
from jax.sharding import Mesh
from jax.sharding import PartitionSpec as P

HD = 128
ROPE = 64
QUEUE = 42
GROUPS = ((1, 3), (2, 0))
BF = jnp.bfloat16
F32 = jnp.float32


def contract_last(left, right):
    return lax.dot_general(left, right, (((1,), (1,)), ((), ())), preferred_element_type=F32)


def flip(array, axis, bit):
    size = lax.axis_size(axis)
    return lax.ppermute(array, axis, [(i, i ^ bit) for i in range(size)])


def shift(array, axis, step):
    size = lax.axis_size(axis)
    return lax.ppermute(array, axis, [(i, (i + step) % size) for i in range(size)])


def attention_kernel(row_ref, query_ref, latent_ref, weight_ref, out_ref, top, total, acc):
    step = pl.program_id(0)
    own = row_ref[0]
    rows = query_ref.shape[1]
    keys = latent_ref.shape[0]
    tile = 128

    @pl.when(step == 0)
    def _():
        top[...] = jnp.full(top.shape, -1e30, F32)
        total[...] = jnp.zeros(total.shape, F32)
        acc[...] = jnp.zeros(acc.shape, F32)

    def work(masked):
        lat = latent_ref[:, : 4 * HD]
        rope = latent_ref[:, 4 * HD :]
        for head in range(2):
            weight = weight_ref[:, 2 * HD * head : 2 * HD * (head + 1)]
            both = jnp.dot(lat, weight, preferred_element_type=F32).astype(BF)
            key = jnp.concatenate([both[:, :HD], rope], axis=1)
            value = both[:, HD:]
            for part in range(rows // tile):
                at = slice(part * tile, (part + 1) * tile)
                scores = contract_last(query_ref[head, at, :], key) * ((HD + ROPE) ** (-0.5))
                if masked:
                    row = lax.broadcasted_iota(jnp.int32, (tile, keys), 0) + part * tile
                    col = lax.broadcasted_iota(jnp.int32, (tile, keys), 1)
                    scores = jnp.where(row >= col, scores, -1e30)
                before = top[head, at, :]
                now = jnp.maximum(before, jnp.max(scores, axis=1, keepdims=True))
                scale = jnp.exp(before - now)
                expo = jnp.exp(scores - now[:, :1])
                total[head, at, :] = total[head, at, :] * scale + jnp.sum(
                    expo, axis=1, keepdims=True
                )
                acc[head, at, :] = acc[head, at, :] * scale + jnp.dot(
                    expo.astype(BF), value, preferred_element_type=F32
                )
                top[head, at, :] = now

    @pl.when(step < own)
    def _():
        work(False)

    @pl.when(step == own)
    def _():
        work(True)

    @pl.when(step == pl.num_programs(0) - 1)
    def _():
        for head in range(2):
            out_ref[:, HD * head : HD * (head + 1)] = (acc[head] / total[head]).astype(BF)


def attention(own, head_query, latents, w_ukv):
    heads, rows, width = head_query.shape
    length, depth = latents.shape
    steps = length // rows
    return pl.pallas_call(
        attention_kernel,
        out_shape=jax.ShapeDtypeStruct((rows, heads * HD), BF),
        grid_spec=pltpu.PrefetchScalarGridSpec(
            num_scalar_prefetch=1,
            grid=(steps,),
            in_specs=[
                pl.BlockSpec((heads, rows, width), lambda j, own: (0, 0, 0)),
                pl.BlockSpec((rows, depth), lambda j, own: (jnp.minimum(j, own[0]), 0)),
                pl.BlockSpec(w_ukv.shape, lambda j, own: (0, 0)),
            ],
            out_specs=pl.BlockSpec((rows, heads * HD), lambda j, own: (0, 0)),
            scratch_shapes=[
                pltpu.VMEM((heads, rows, HD), F32),
                pltpu.VMEM((heads, rows, HD), F32),
                pltpu.VMEM((heads, rows, HD), F32),
            ],
        ),
        compiler_params=pltpu.CompilerParams(vmem_limit_bytes=32 * 2**20),
        cost_estimate=pl.CostEstimate(
            flops=2 * rows * length * 640 + 2 * length * 512 * 512,
            bytes_accessed=2 * length * depth + 2 * rows * 1024,
            transcendentals=heads * rows * length,
        ),
    )(own.reshape(1), head_query, latents, w_ukv)


def body(
    moe_grad,
    saved_act,
    route_prob,
    expert_ids,
    w_gate,
    w_up,
    w_down,
    queries,
    latent,
    rope_keys,
    w_ukv,
    latent_b,
    grad_kv_b,
):
    tokens, width = moe_grad.shape
    top_count = expert_ids.shape[1]
    share = saved_act.shape[3]
    xi, hi, zi, yi, ci = (lax.axis_index(name) for name in ("x", "h", "z", "y", "c"))
    experts = 32
    rows_y = 8 * QUEUE

    joined = jnp.concatenate([latent, rope_keys], axis=1)
    latents = lax.all_gather(joined, ("z", "y", "c"), axis=0, tiled=True)
    ukv_part = lax.dot_general(
        latent_b, grad_kv_b, (((0,), (0,)), ((), ())), preferred_element_type=F32
    ).astype(BF)
    ukv_grad = lax.psum_scatter(ukv_part, ("x", "h"), scatter_dimension=0, tiled=True).astype(F32)

    hit = expert_ids[:, :, None] == jnp.arange(experts, dtype=jnp.int32)
    probs = jnp.sum(jnp.where(hit, route_prob[:, :, None].astype(F32), 0.0), axis=1)
    probs_t = probs.T.astype(BF)

    def near(array):
        far = flip(array, "z", 2)
        pair = jnp.stack([array, far])
        other = flip(pair, "z", 1)
        own = jnp.stack([pair[0], other[0], pair[1], other[1]])
        return jnp.stack([own, flip(own, "c", 1)])

    near_probs = near(probs_t)
    near_tokens = near(moe_grad).reshape(8 * tokens, width)

    picked = jnp.stack(
        [
            lax.dynamic_index_in_dim(near_probs, zi * 8 + ((yi + s) % 4) * 2 + ci, 2, False)
            for s in range(4)
        ]
    ).reshape(4, 8, tokens)
    member = picked > 0
    before = jnp.triu(jnp.ones((tokens, tokens), BF), 1)
    spot = lax.dot_general(
        member.astype(BF).reshape(32, tokens),
        before,
        (((1,), (0,)), ((), ())),
        preferred_element_type=F32,
    ).astype(jnp.int32)
    flips = jnp.arange(8, dtype=jnp.int32)
    block = ((flips % 4) ^ zi) * 2 + ((flips // 4) ^ ci)
    slot = spot.reshape(4, 8, tokens) + block[None, :, None] * QUEUE
    slot = jnp.where(member, slot, -1).reshape(4, 1, 8 * tokens)
    chosen = slot == jnp.arange(rows_y, dtype=jnp.int32)[None, :, None]
    picked = picked.reshape(4, 1, 8 * tokens)

    sent = [
        jnp.dot(
            jnp.where(chosen[s], picked[s], jnp.zeros((), BF)),
            near_tokens,
            preferred_element_type=F32,
        ).astype(BF)
        for s in range(4)
    ]
    arrived = [sent[0]] + [shift(sent[s], "y", s) for s in (1, 2, 3)]

    member_all = (probs > 0).astype(BF)
    spot_all = lax.dot_general(
        jnp.tril(jnp.ones((tokens, tokens), BF), -1),
        member_all,
        (((1,), (0,)), ((), ())),
        preferred_element_type=F32,
    )
    spot_own = jnp.sum(jnp.where(hit, spot_all[:, None, :], 0.0), axis=2).astype(jnp.int32)
    order = ((expert_ids // 2) % 4) * 8 + (expert_ids // 8) * 2 + expert_ids % 2
    target = (order * QUEUE + spot_own).reshape(1, tokens * top_count)
    place = (target == jnp.arange(experts * QUEUE, dtype=jnp.int32)[:, None]).astype(BF)
    send_saved = jnp.dot(
        place,
        saved_act.reshape(tokens * top_count, 2 * share),
        preferred_element_type=F32,
    ).astype(BF)
    got_saved = lax.all_to_all(
        send_saved.reshape(experts, QUEUE, 2, share),
        ("y", "z", "c"),
        split_axis=0,
        concat_axis=0,
        tiled=True,
    ).reshape(4, rows_y, 2, share)

    down = w_down[0].reshape(4, 2 * share, width)
    down_rel = [lax.dynamic_index_in_dim(down, (xi + s) % 4, 0, False) for s in range(4)]

    def weight_piece(s, flipped):
        at = (((xi - s) % 4) * 2 + (hi ^ flipped)) * share
        return jnp.concatenate(
            [
                lax.dynamic_slice_in_dim(w_gate[0], at, share, 1),
                lax.dynamic_slice_in_dim(w_up[0], at, share, 1),
            ],
            axis=1,
        )

    pieces = [(s, flipped) for s in range(4) for flipped in range(2)]
    weight_rel = jnp.concatenate([weight_piece(*piece) for piece in pieces], axis=1)

    returned = [None] * 4
    for group in GROUPS:
        rows = jnp.concatenate([arrived[s] for s in group], axis=0)
        saved = jnp.concatenate(
            [lax.dynamic_index_in_dim(got_saved, (yi - s) % 4, 0, False) for s in group], axis=0
        )
        parts = [contract_last(rows, down_rel[s]) for s in range(4)]
        total = parts[0]
        for s in (1, 3, 2):
            total = total + shift(parts[s].astype(BF), "x", s).astype(F32)
        mine = lax.dynamic_slice_in_dim(total, hi * share, share, 1)
        theirs = lax.dynamic_slice_in_dim(total, (1 - hi) * share, share, 1)
        hidden = mine + flip(theirs.astype(BF), "h", 1).astype(F32)

        gate_pre = saved[:, 0].astype(F32)
        up_pre = saved[:, 1].astype(F32)
        sigmoid_gate = jax.nn.sigmoid(gate_pre)
        grad_gate = (
            hidden * up_pre * sigmoid_gate * (1.0 + gate_pre * (1.0 - sigmoid_gate))
        ).astype(BF)
        grad_up = (hidden * gate_pre * sigmoid_gate).astype(BF)
        grads = jnp.concatenate([grad_gate, grad_up], axis=1)

        pair = jnp.stack([grads, flip(grads, "h", 1)])
        left = shift(pair, "x", 1)
        right = shift(pair, "x", -1)
        across_a = shift(left[0], "x", 1)
        across_b = shift(right[1], "x", -1)
        gathered = [pair[0], pair[1], left[0], left[1], across_a, across_b, right[0], right[1]]
        contribution = contract_last(jnp.concatenate(gathered, axis=1), weight_rel).astype(BF)
        for i, s in enumerate(group):
            piece = contribution[i * rows_y : (i + 1) * rows_y]
            returned[s] = shift(piece, "y", -s) if s else piece

    gather_all = chosen.astype(BF)
    dense = sum(
        lax.dot_general(
            gather_all[s], returned[s], (((0,), (0,)), ((), ())), preferred_element_type=F32
        )
        for s in range(4)
    ).reshape(2, 4, tokens, width)
    sums = dense[0] + flip(dense[1].astype(BF), "c", 1).astype(F32)
    near_sums = flip(jnp.stack([sums[1], sums[3]]).astype(BF), "z", 1).astype(F32)
    first = sums[0] + near_sums[0]
    second = sums[2] + near_sums[1]
    moe_input_grad = (first + flip(second.astype(BF), "z", 2).astype(F32)).astype(BF)

    head_query = queries.reshape(queries.shape[0], 2, HD + ROPE).transpose(1, 0, 2)
    attn_out = attention(xi * 2 + hi, head_query, latents, w_ukv)
    return (moe_input_grad, attn_out, ukv_grad)


def solution(mesh):
    fine = Mesh(mesh.devices.reshape(4, 2, 4, 4, 2), ("x", "h", "z", "y", "c"))
    dp = ("x", "h")
    expert = ("z", "y", "c")
    in_specs = (
        P(expert, dp),
        P(expert, None, None, dp),
        P(expert, None),
        P(expert, None),
        P(expert, dp, None),
        P(expert, dp, None),
        P(expert, None, dp),
        P(dp, expert),
        P(expert, None),
        P(expert, None),
        P(None, expert),
        P(dp, None),
        P(dp, expert),
    )
    out_specs = (P(expert, dp), P(dp, expert), P(dp, expert))
    return jax.shard_map(body, mesh=fine, in_specs=in_specs, out_specs=out_specs, check_vma=False)
```

```python
import jax
import jax.numpy as jnp
from jax import lax
from jax.experimental import pallas as pl
from jax.experimental.pallas import tpu as pltpu
from jax.sharding import Mesh
from jax.sharding import PartitionSpec as P

HD = 128
ROPE = 64
QUEUE = 42
PADDED = 48
GROUPS = ((1, 3), (2, 0))
LOG2E = 1.4426950408889634
BF = jnp.bfloat16
F32 = jnp.float32


def contract_last(left, right):
    return lax.dot_general(left, right, (((1,), (1,)), ((), ())), preferred_element_type=F32)


def flip(array, axis, bit):
    size = lax.axis_size(axis)
    return lax.ppermute(array, axis, [(i, i ^ bit) for i in range(size)])


def shift(array, axis, step):
    size = lax.axis_size(axis)
    return lax.ppermute(array, axis, [(i, (i + step) % size) for i in range(size)])


def tie(value, *others):
    return lax.optimization_barrier((value, *others))[0]


def whole(shape):
    return pl.BlockSpec(shape, lambda *_: (0,) * len(shape))


def attention_kernel(place_ref, query_ref, *refs):
    latent_refs, (weight_ref, out_ref, top, total, acc) = refs[:4], refs[4:]
    step = pl.program_id(0)
    own = place_ref[0]
    rows = query_ref.shape[1]
    size = latent_refs[0].shape[2]
    keys = 4 * size
    tile = min(256, rows)
    factor = (HD + ROPE) ** (-0.5) * LOG2E

    @pl.when(step == 0)
    def _():
        top[...] = jnp.full(top.shape, -1e30, F32)
        total[...] = jnp.zeros(total.shape, F32)
        acc[...] = jnp.zeros(acc.shape, F32)

    def work(masked):
        joined = jnp.concatenate([ref[0, 0] for ref in latent_refs], axis=0)
        both = jnp.dot(joined[:, : 4 * HD], weight_ref[...], preferred_element_type=F32)
        key = jnp.concatenate(
            [both[:, :HD].astype(BF), joined[:, 4 * HD : 4 * HD + ROPE]], axis=1
        )
        value = both[:, HD:].T.astype(BF)
        for part in range(rows // tile):
            at = slice(part * tile, (part + 1) * tile)
            scores = jnp.dot(key, query_ref[:, at], preferred_element_type=F32)
            if masked:
                line = lax.broadcasted_iota(jnp.int32, (size, tile), 0)
                row = jnp.concatenate(
                    [
                        line + (pair * 2 * size + (place_ref[3] ^ flipped) * size)
                        for pair in range(2)
                        for flipped in range(2)
                    ],
                    axis=0,
                )
                col = lax.broadcasted_iota(jnp.int32, (keys, tile), 1) + part * tile
                scores = jnp.where(row <= col, scores, -1e30)
            before = top[:, at]
            now = jnp.maximum(before, jnp.max(scores, axis=0, keepdims=True))
            scale = jnp.exp2((before - now) * factor)
            expo = jnp.exp2((scores - now) * factor)
            total[:, at] = total[:, at] * scale + jnp.sum(expo, axis=0, keepdims=True)
            acc[:, at] = acc[:, at] * scale + jnp.dot(
                value, expo.astype(BF), preferred_element_type=F32
            )
            top[:, at] = now

    @pl.when(step < own)
    def _():
        work(False)

    @pl.when(step == own)
    def _():
        work(True)

    @pl.when(step == pl.num_programs(0) - 1)
    def _():
        out_ref[...] = (acc[...] / total[...]).T.astype(BF)


def attention(place, head_query, near_latents, far_latents, weight):
    width, rows = head_query.shape
    _, _, size, depth = near_latents.shape
    steps = 8

    def latent_spec(pair):
        def index(j, place):
            step = jnp.minimum(j, place[0])
            return (lax.rem(step, 2) * 2 + pair, lax.div(step, 2) ^ place[1], 0, 0)

        return pl.BlockSpec((1, 1, size, depth), index)

    return pl.pallas_call(
        attention_kernel,
        out_shape=jax.ShapeDtypeStruct((rows, HD), BF),
        grid_spec=pltpu.PrefetchScalarGridSpec(
            num_scalar_prefetch=1,
            grid=(steps,),
            in_specs=[
                whole((width, rows)),
                latent_spec(0),
                latent_spec(0),
                latent_spec(1),
                latent_spec(1),
                whole(weight.shape),
            ],
            out_specs=whole((rows, HD)),
            scratch_shapes=[
                pltpu.VMEM((1, rows), F32),
                pltpu.VMEM((1, rows), F32),
                pltpu.VMEM((HD, rows), F32),
            ],
        ),
        compiler_params=pltpu.CompilerParams(vmem_limit_bytes=32 * 2**20),
        cost_estimate=pl.CostEstimate(
            flops=2 * steps * rows * (rows * 320 + 512 * 256),
            bytes_accessed=2 * steps * rows * depth,
            transcendentals=steps * rows * rows,
        ),
    )(
        place,
        head_query,
        near_latents,
        far_latents,
        near_latents,
        far_latents,
        weight,
    )


def hidden_kernel(count, place_ref, *refs):
    rows_refs, weight_ref, out_refs = refs[:count], refs[count], refs[-4:]
    size = rows_refs[0].shape[0]
    cols = out_refs[0].shape[1]
    for s in range(4):
        at = pl.multiple_of(lax.rem(place_ref[0] + s, 4) * cols, cols)
        weight = weight_ref[pl.ds(at, cols), :]
        for i in range(count):
            out_refs[s][i * size : (i + 1) * size, :] = contract_last(
                rows_refs[i][...], weight
            ).astype(out_refs[s].dtype)


def hidden_parts(place, rows, weight, *earlier):
    count = len(rows)
    size, width = rows[0].shape
    hidden = weight.shape[0]
    shape = (count * size, hidden // 4)
    kinds = [F32, BF, BF, BF]
    return pl.pallas_call(
        lambda *refs: hidden_kernel(count, *refs),
        out_shape=[jax.ShapeDtypeStruct(shape, kind) for kind in kinds],
        grid_spec=pltpu.PrefetchScalarGridSpec(
            num_scalar_prefetch=1,
            grid=(1,),
            in_specs=[whole((size, width))] * count
            + [whole(weight.shape)]
            + [pl.BlockSpec(memory_space=pl.ANY)] * len(earlier),
            out_specs=[whole(shape)] * 4,
        ),
        compiler_params=pltpu.CompilerParams(vmem_limit_bytes=32 * 2**20),
        cost_estimate=pl.CostEstimate(
            flops=2 * count * size * width * hidden,
            bytes_accessed=2 * count * size * (width + hidden) + 2 * width * hidden,
            transcendentals=0,
        ),
    )(place.reshape(1), *rows, weight, *earlier)


def factor_kernel(place_ref, saved_ref, gate_ref, up_ref):
    rows = gate_ref.shape[1]
    share = saved_ref.shape[2] // 2
    slot = lax.broadcasted_iota(jnp.int32, (rows, saved_ref.shape[1]), 0)
    spot = lax.broadcasted_iota(jnp.int32, (rows, saved_ref.shape[1]), 1)
    block = lax.div(slot, QUEUE)
    keep = (block * PADDED + (slot - block * QUEUE) == spot).astype(BF)
    for s in range(4):
        source = lax.rem(place_ref[0] + 4 - s, 4)
        saved = jnp.dot(keep, saved_ref[source], preferred_element_type=F32)
        gate_pre, up_pre = saved[:, :share], saved[:, share:]
        sigmoid_gate = 1.0 / (1.0 + jnp.exp(-gate_pre))
        gate_ref[s] = up_pre * sigmoid_gate * (1.0 + gate_pre * (1.0 - sigmoid_gate))
        up_ref[s] = gate_pre * sigmoid_gate


def factors(place, saved, rows):
    shape = (4, rows, saved.shape[2] // 2)
    return pl.pallas_call(
        factor_kernel,
        out_shape=[jax.ShapeDtypeStruct(shape, F32)] * 2,
        grid_spec=pltpu.PrefetchScalarGridSpec(
            num_scalar_prefetch=1,
            grid=(1,),
            in_specs=[whole(saved.shape)],
            out_specs=[whole(shape)] * 2,
        ),
        compiler_params=pltpu.CompilerParams(vmem_limit_bytes=24 * 2**20),
        cost_estimate=pl.CostEstimate(
            flops=8 * rows * saved.shape[1] * saved.shape[2],
            bytes_accessed=2 * saved.size + 32 * rows * shape[2],
            transcendentals=4 * rows * shape[2],
        ),
    )(place.reshape(1), saved)


def combine_kernel(chosen_ref, rows_ref, *refs):
    refs[-1][...] = lax.dot_general(
        chosen_ref[...], rows_ref[...], (((0,), (0,)), ((), ())), preferred_element_type=F32
    )


def combine(chosen, rows, *earlier):
    shape = (chosen.shape[1], rows.shape[1])
    return pl.pallas_call(
        combine_kernel,
        out_shape=jax.ShapeDtypeStruct(shape, F32),
        grid=(1,),
        in_specs=[whole(chosen.shape), whole(rows.shape)]
        + [pl.BlockSpec(memory_space=pl.ANY)] * len(earlier),
        out_specs=whole(shape),
        compiler_params=pltpu.CompilerParams(vmem_limit_bytes=24 * 2**20),
        cost_estimate=pl.CostEstimate(
            flops=2 * shape[0] * rows.size,
            bytes_accessed=2 * (chosen.size + rows.size) + 4 * shape[0] * shape[1],
            transcendentals=0,
        ),
    )(chosen, rows, *earlier)


def input_kernel(
    count, place_ref, own_ref, left_ref, a_ref, b_ref, right_ref, gate_ref, up_ref, *rest
):
    out_refs = rest[-count:]
    size = out_refs[0].shape[0]
    cols = own_ref.shape[2] // 2
    width = gate_ref.shape[0]
    pieces = [
        own_ref.at[0],
        own_ref.at[1],
        left_ref.at[0],
        left_ref.at[1],
        a_ref,
        b_ref,
        right_ref.at[0],
        right_ref.at[1],
    ]
    sides = (place_ref[1], 1 - place_ref[1])
    starts = [
        pl.multiple_of((lax.rem(place_ref[0] + 4 - s, 4) * 2 + side) * cols, cols)
        for s in range(4)
        for side in sides
    ]
    for first in range(0, width, 256):
        last = min(first + 256, width)
        weight = jnp.concatenate(
            [ref[first:last, pl.ds(start, cols)] for start in starts for ref in (gate_ref, up_ref)],
            axis=1,
        )
        for i in range(count):
            at = slice(i * size, (i + 1) * size)
            left = jnp.concatenate([ref[at, :] for ref in pieces], axis=1)
            out_refs[i][:, first:last] = contract_last(left, weight).astype(BF)


def input_parts(place, count, own, left, across_a, across_b, right, gate, up, *earlier):
    rows = own.shape[1]
    size = rows // count
    width, hidden = gate.shape
    arrays = (own, left, across_a, across_b, right, gate, up)
    return pl.pallas_call(
        lambda *refs: input_kernel(count, *refs),
        out_shape=[jax.ShapeDtypeStruct((size, width), BF)] * count,
        grid_spec=pltpu.PrefetchScalarGridSpec(
            num_scalar_prefetch=1,
            grid=(1,),
            in_specs=[whole(array.shape) for array in arrays]
            + [pl.BlockSpec(memory_space=pl.ANY)] * len(earlier),
            out_specs=[whole((size, width))] * count,
        ),
        compiler_params=pltpu.CompilerParams(vmem_limit_bytes=48 * 2**20),
        cost_estimate=pl.CostEstimate(
            flops=4 * rows * width * hidden,
            bytes_accessed=2 * rows * (width + 2 * hidden) + 4 * width * hidden,
            transcendentals=0,
        ),
    )(place, *arrays, *earlier)


def body(
    moe_grad,
    saved_act,
    route_prob,
    expert_ids,
    w_gate,
    w_up,
    w_down,
    queries,
    latent,
    rope_keys,
    w_ukv,
    latent_b,
    grad_kv_b,
):
    tokens, width = moe_grad.shape
    top_count = expert_ids.shape[1]
    share = saved_act.shape[3]
    xi, hi, zi, yi, ci = (lax.axis_index(name) for name in ("x", "h", "z", "y", "c"))
    experts = 32
    rows_y = 8 * QUEUE

    ukv_part = lax.dot_general(
        latent_b, grad_kv_b, (((0,), (0,)), ((), ())), preferred_element_type=F32
    ).astype(BF)
    hit = expert_ids[:, :, None] == jnp.arange(experts, dtype=jnp.int32)
    probs = jnp.sum(jnp.where(hit, route_prob[:, :, None].astype(F32), 0.0), axis=1)
    member_all = (probs > 0).astype(BF)
    spot_all = lax.dot_general(
        jnp.tril(jnp.ones((tokens, tokens), BF), -1),
        member_all,
        (((1,), (0,)), ((), ())),
        preferred_element_type=F32,
    )
    spot_own = jnp.sum(jnp.where(hit, spot_all[:, None, :], 0.0), axis=2).astype(jnp.int32)
    order = ((expert_ids // 2) % 4) * 8 + (expert_ids // 8) * 2 + expert_ids % 2
    target = (order * PADDED + spot_own).reshape(1, tokens * top_count)
    place = (target == jnp.arange(experts * PADDED, dtype=jnp.int32)[:, None]).astype(BF)
    send_saved = jnp.dot(
        place,
        saved_act.reshape(tokens * top_count, 2 * share),
        preferred_element_type=F32,
    ).astype(BF)

    near_a = (moe_grad, probs.T.astype(BF))
    far = [flip(array, "z", 2) for array in near_a]
    near_b = lax.optimization_barrier(
        tuple(jnp.stack(both) for both in zip(near_a, far)) + (send_saved, ukv_part)
    )
    near_b, send_saved, ukv_part = near_b[:2], near_b[2], near_b[3]
    near_c = [
        jnp.stack([pair[0], other[0], pair[1], other[1]])
        for pair, other in zip(near_b, [flip(array, "z", 1) for array in near_b])
    ]
    near_tokens, near_probs = lax.optimization_barrier(
        tuple(jnp.stack([array, flip(array, "c", 1)]) for array in near_c)
    )
    near_tokens = near_tokens.reshape(8 * tokens, width)
    got_saved = lax.all_to_all(
        send_saved, ("y", "z", "c"), split_axis=0, concat_axis=0, tiled=True
    ).reshape(4, 8 * PADDED, 2 * share)
    ukv_rows = ukv_part.shape[0] // 8
    ukv_all = lax.all_to_all(ukv_part, "x", split_axis=0, concat_axis=0, tiled=True)
    ukv_pair = jnp.sum(ukv_all.astype(F32).reshape(4, 2 * ukv_rows, ukv_part.shape[1]), axis=0)
    ukv_own = lax.dynamic_slice_in_dim(ukv_pair, hi * ukv_rows, ukv_rows, 0)
    ukv_far = lax.dynamic_slice_in_dim(ukv_pair, (1 - hi) * ukv_rows, ukv_rows, 0)
    ukv_grad = ukv_own + flip(ukv_far.astype(BF), "h", 1).astype(F32)

    picked = jnp.stack(
        [
            lax.dynamic_index_in_dim(near_probs, zi * 8 + ((yi + s) % 4) * 2 + ci, 2, False)
            for s in range(4)
        ]
    ).reshape(4, 8, tokens)
    member = picked > 0
    before = jnp.triu(jnp.ones((tokens, tokens), BF), 1)
    spot = lax.dot_general(
        member.astype(BF).reshape(32, tokens),
        before,
        (((1,), (0,)), ((), ())),
        preferred_element_type=F32,
    ).astype(jnp.int32)
    flips = jnp.arange(8, dtype=jnp.int32)
    block = ((flips % 4) ^ zi) * 2 + ((flips // 4) ^ ci)
    slot = spot.reshape(4, 8, tokens) + block[None, :, None] * QUEUE
    slot = jnp.where(member, slot, -1).reshape(4, 1, 8 * tokens)
    chosen = slot == jnp.arange(rows_y, dtype=jnp.int32)[None, :, None]
    picked = picked.reshape(4, 1, 8 * tokens)

    sent = [
        jnp.dot(
            jnp.where(chosen[s], picked[s], jnp.zeros((), BF)),
            near_tokens,
            preferred_element_type=F32,
        ).astype(BF)
        for s in range(4)
    ]
    arrived = [sent[0]] + [shift(sent[s], "y", s) for s in (1, 2, 3)]

    joined = jnp.concatenate(
        [latent, rope_keys, jnp.zeros((tokens, HD - ROPE), BF)], axis=1
    )
    lat_pair = tie(joined, *arrived)
    lat_pair = jnp.stack([lat_pair, flip(lat_pair, "z", 2)])
    lat_other = flip(lat_pair, "z", 1)
    lat_z = jnp.stack([lat_pair[0], lat_other[0], lat_pair[1], lat_other[1]])
    near_latents = lax.all_gather(lat_z, "y", axis=0)
    far_latents = flip(near_latents, "c", 1)

    gate_factor, up_factor = factors(yi.astype(jnp.int32), got_saved, rows_y)
    here = jnp.stack([xi, hi]).astype(jnp.int32)

    head_query = queries.reshape(queries.shape[0], 2, HD + ROPE).transpose(1, 2, 0)

    def attend(head):
        return attention(
            jnp.stack([xi * 2 + hi, zi, yi, ci]).astype(jnp.int32),
            head_query[head],
            near_latents,
            far_latents,
            w_ukv[:, 2 * HD * head : 2 * HD * (head + 1)],
        )

    returned = [None] * 4
    attn = [attend(0), attend(1)]
    for number, group in enumerate(GROUPS):
        earlier = [ukv_grad] if number else [arrived[2]]
        parts = hidden_parts(xi, [arrived[s] for s in group], w_down[0], *earlier)
        total = parts[0]
        for s in (1, 3, 2):
            total = total + shift(parts[s], "x", s).astype(F32)
        own_total = lax.dynamic_slice_in_dim(total, hi * share, share, 1)
        far_total = lax.dynamic_slice_in_dim(total, (1 - hi) * share, share, 1)
        hidden = own_total + flip(far_total.astype(BF), "h", 1).astype(F32)
        grads = jnp.concatenate(
            [
                (hidden * jnp.concatenate([array[s] for s in group], axis=0)).astype(BF)
                for array in (gate_factor, up_factor)
            ],
            axis=1,
        )
        pair = jnp.stack([grads, flip(grads, "h", 1)])
        left = shift(pair, "x", 1)
        right = shift(pair, "x", -1)
        across_a = shift(left[0], "x", 1)
        across_b = shift(right[1], "x", -1)
        ordered = (attn[0],) if number else ()
        pieces = input_parts(
            here,
            len(group),
            pair,
            left,
            across_a,
            across_b,
            right,
            w_gate[0],
            w_up[0],
            *ordered,
        )
        for s, piece in zip(group, pieces):
            returned[s] = shift(piece, "y", -s) if s else piece

    gather_all = chosen.astype(BF)
    dense = sum(
        lax.dot_general(
            gather_all[s], returned[s], (((0,), (0,)), ((), ())), preferred_element_type=F32
        )
        for s in (0, 1, 3)
    )
    dense = (dense + combine(gather_all[2], returned[2], attn[1])).reshape(2, 4, tokens, width)
    sums = dense[0] + flip(dense[1].astype(BF), "c", 1).astype(F32)
    near_sums = flip(jnp.stack([sums[1], sums[3]]).astype(BF), "z", 1).astype(F32)
    first = sums[0] + near_sums[0]
    second = (sums[2] + near_sums[1]).astype(BF)
    moe_input_grad = (first + flip(second, "z", 2).astype(F32)).astype(BF)
    attn_out = jnp.concatenate(attn, axis=1)
    return (moe_input_grad, attn_out, ukv_grad)


def solution(mesh):
    fine = Mesh(mesh.devices.reshape(4, 2, 4, 4, 2), ("x", "h", "z", "y", "c"))
    dp = ("x", "h")
    expert = ("z", "y", "c")
    in_specs = (
        P(expert, dp),
        P(expert, None, None, dp),
        P(expert, None),
        P(expert, None),
        P(expert, dp, None),
        P(expert, dp, None),
        P(expert, None, dp),
        P(dp, expert),
        P(expert, None),
        P(expert, None),
        P(None, expert),
        P(dp, None),
        P(dp, expert),
    )
    out_specs = (P(expert, dp), P(dp, expert), P(dp, expert))
    return jax.shard_map(body, mesh=fine, in_specs=in_specs, out_specs=out_specs, check_vma=False)
```

```python
import jax
import jax.numpy as jnp
from jax import lax
from jax.experimental import pallas as pl
from jax.experimental.pallas import tpu as pltpu
from jax.sharding import Mesh
from jax.sharding import PartitionSpec as P

HD = 128
ROPE = 64
QUEUE = 42
PADDED = 48
GROUPS = ((1, 3), (2, 0))
LOG2E = 1.4426950408889634
BF = jnp.bfloat16
F32 = jnp.float32


def contract_last(left, right):
    return lax.dot_general(left, right, (((1,), (1,)), ((), ())), preferred_element_type=F32)


def flip(array, axis, bit):
    size = lax.axis_size(axis)
    return lax.ppermute(array, axis, [(i, i ^ bit) for i in range(size)])


def shift(array, axis, step):
    size = lax.axis_size(axis)
    return lax.ppermute(array, axis, [(i, (i + step) % size) for i in range(size)])


def tie(value, *others):
    return lax.optimization_barrier((value, *others))[0]


def whole(shape):
    return pl.BlockSpec(shape, lambda *_: (0,) * len(shape))


def attention_kernel(place_ref, query_ref, *refs):
    latent_refs, (weight_ref, out_ref, top, total, acc) = refs[:4], refs[4:]
    step = pl.program_id(0)
    own = place_ref[0]
    rows = query_ref.shape[1]
    size = latent_refs[0].shape[2]
    keys = 4 * size
    tile = min(256, rows)
    factor = (HD + ROPE) ** (-0.5) * LOG2E

    @pl.when(step == 0)
    def _():
        top[...] = jnp.full(top.shape, -1e30, F32)
        total[...] = jnp.zeros(total.shape, F32)
        acc[...] = jnp.zeros(acc.shape, F32)

    def work(masked):
        joined = jnp.concatenate([ref[0, 0] for ref in latent_refs], axis=0)
        both = jnp.dot(joined[:, : 4 * HD], weight_ref[...], preferred_element_type=F32)
        key = jnp.concatenate(
            [both[:, :HD].astype(BF), joined[:, 4 * HD : 4 * HD + ROPE]], axis=1
        )
        value = both[:, HD:].T.astype(BF)
        for part in range(rows // tile):
            at = slice(part * tile, (part + 1) * tile)
            scores = jnp.dot(key, query_ref[:, at], preferred_element_type=F32)
            if masked:
                line = lax.broadcasted_iota(jnp.int32, (size, tile), 0)
                row = jnp.concatenate(
                    [
                        line + (pair * 2 * size + (place_ref[3] ^ flipped) * size)
                        for pair in range(2)
                        for flipped in range(2)
                    ],
                    axis=0,
                )
                col = lax.broadcasted_iota(jnp.int32, (keys, tile), 1) + part * tile
                scores = jnp.where(row <= col, scores, -1e30)
            before = top[:, at]
            now = jnp.maximum(before, jnp.max(scores, axis=0, keepdims=True))
            scale = jnp.exp2((before - now) * factor)
            expo = jnp.exp2((scores - now) * factor)
            total[:, at] = total[:, at] * scale + jnp.sum(expo, axis=0, keepdims=True)
            acc[:, at] = acc[:, at] * scale + jnp.dot(
                value, expo.astype(BF), preferred_element_type=F32
            )
            top[:, at] = now

    @pl.when(step < own)
    def _():
        work(False)

    @pl.when(step == own)
    def _():
        work(True)

    @pl.when(step == pl.num_programs(0) - 1)
    def _():
        out_ref[...] = (acc[...] / total[...]).T.astype(BF)


def attention(place, head_query, near_latents, far_latents, weight):
    width, rows = head_query.shape
    _, _, size, depth = near_latents.shape
    steps = 8

    def latent_spec(pair):
        def index(j, place):
            step = jnp.minimum(j, place[0])
            return (lax.div(step, 2), lax.rem(step, 2) * 2 + pair, 0, 0)

        return pl.BlockSpec((1, 1, size, depth), index)

    return pl.pallas_call(
        attention_kernel,
        out_shape=jax.ShapeDtypeStruct((rows, HD), BF),
        grid_spec=pltpu.PrefetchScalarGridSpec(
            num_scalar_prefetch=1,
            grid=(steps,),
            in_specs=[
                whole((width, rows)),
                latent_spec(0),
                latent_spec(0),
                latent_spec(1),
                latent_spec(1),
                whole(weight.shape),
            ],
            out_specs=whole((rows, HD)),
            scratch_shapes=[
                pltpu.VMEM((1, rows), F32),
                pltpu.VMEM((1, rows), F32),
                pltpu.VMEM((HD, rows), F32),
            ],
        ),
        compiler_params=pltpu.CompilerParams(vmem_limit_bytes=32 * 2**20),
        cost_estimate=pl.CostEstimate(
            flops=2 * steps * rows * (rows * 320 + 512 * 256),
            bytes_accessed=2 * steps * rows * depth,
            transcendentals=steps * rows * rows,
        ),
    )(
        place,
        head_query,
        near_latents,
        far_latents,
        near_latents,
        far_latents,
        weight,
    )


def hidden_kernel(count, place_ref, *refs):
    rows_refs, weight_ref, out_refs = refs[:count], refs[count], refs[-4:]
    size = rows_refs[0].shape[0]
    cols = out_refs[0].shape[1]
    for s in range(4):
        at = pl.multiple_of(lax.rem(place_ref[0] + s, 4) * cols, cols)
        weight = weight_ref[pl.ds(at, cols), :]
        for i in range(count):
            out_refs[s][i * size : (i + 1) * size, :] = contract_last(
                rows_refs[i][...], weight
            ).astype(out_refs[s].dtype)


def hidden_parts(place, rows, weight, *earlier):
    count = len(rows)
    size, width = rows[0].shape
    hidden = weight.shape[0]
    shape = (count * size, hidden // 4)
    kinds = [F32, BF, BF, BF]
    return pl.pallas_call(
        lambda *refs: hidden_kernel(count, *refs),
        out_shape=[jax.ShapeDtypeStruct(shape, kind) for kind in kinds],
        grid_spec=pltpu.PrefetchScalarGridSpec(
            num_scalar_prefetch=1,
            grid=(1,),
            in_specs=[whole((size, width))] * count
            + [whole(weight.shape)]
            + [pl.BlockSpec(memory_space=pl.ANY)] * len(earlier),
            out_specs=[whole(shape)] * 4,
        ),
        compiler_params=pltpu.CompilerParams(vmem_limit_bytes=32 * 2**20),
        cost_estimate=pl.CostEstimate(
            flops=2 * count * size * width * hidden,
            bytes_accessed=2 * count * size * (width + hidden) + 2 * width * hidden,
            transcendentals=0,
        ),
    )(place.reshape(1), *rows, weight, *earlier)


def factor_kernel(place_ref, saved_ref, gate_ref, up_ref):
    rows = gate_ref.shape[1]
    share = saved_ref.shape[2] // 2
    slot = lax.broadcasted_iota(jnp.int32, (rows, saved_ref.shape[1]), 0)
    spot = lax.broadcasted_iota(jnp.int32, (rows, saved_ref.shape[1]), 1)
    block = lax.div(slot, QUEUE)
    keep = (block * PADDED + (slot - block * QUEUE) == spot).astype(BF)
    for s in range(4):
        source = lax.rem(place_ref[0] + 4 - s, 4)
        saved = jnp.dot(keep, saved_ref[source], preferred_element_type=F32)
        gate_pre, up_pre = saved[:, :share], saved[:, share:]
        sigmoid_gate = 1.0 / (1.0 + jnp.exp(-gate_pre))
        gate_ref[s] = up_pre * sigmoid_gate * (1.0 + gate_pre * (1.0 - sigmoid_gate))
        up_ref[s] = gate_pre * sigmoid_gate


def factors(place, saved, rows):
    shape = (4, rows, saved.shape[2] // 2)
    return pl.pallas_call(
        factor_kernel,
        out_shape=[jax.ShapeDtypeStruct(shape, F32)] * 2,
        grid_spec=pltpu.PrefetchScalarGridSpec(
            num_scalar_prefetch=1,
            grid=(1,),
            in_specs=[whole(saved.shape)],
            out_specs=[whole(shape)] * 2,
        ),
        compiler_params=pltpu.CompilerParams(vmem_limit_bytes=24 * 2**20),
        cost_estimate=pl.CostEstimate(
            flops=8 * rows * saved.shape[1] * saved.shape[2],
            bytes_accessed=2 * saved.size + 32 * rows * shape[2],
            transcendentals=4 * rows * shape[2],
        ),
    )(place.reshape(1), saved)


def combine_kernel(chosen_ref, rows_ref, *refs):
    refs[-1][...] = lax.dot_general(
        chosen_ref[...], rows_ref[...], (((0,), (0,)), ((), ())), preferred_element_type=F32
    )


def combine(chosen, rows, *earlier):
    shape = (chosen.shape[1], rows.shape[1])
    return pl.pallas_call(
        combine_kernel,
        out_shape=jax.ShapeDtypeStruct(shape, F32),
        grid=(1,),
        in_specs=[whole(chosen.shape), whole(rows.shape)]
        + [pl.BlockSpec(memory_space=pl.ANY)] * len(earlier),
        out_specs=whole(shape),
        compiler_params=pltpu.CompilerParams(vmem_limit_bytes=24 * 2**20),
        cost_estimate=pl.CostEstimate(
            flops=2 * shape[0] * rows.size,
            bytes_accessed=2 * (chosen.size + rows.size) + 4 * shape[0] * shape[1],
            transcendentals=0,
        ),
    )(chosen, rows, *earlier)


def input_kernel(
    count, place_ref, own_ref, left_ref, a_ref, b_ref, right_ref, gate_ref, up_ref, *rest
):
    out_refs = rest[-count:]
    size = out_refs[0].shape[0]
    cols = own_ref.shape[2] // 2
    width = gate_ref.shape[0]
    pieces = [
        own_ref.at[0],
        own_ref.at[1],
        left_ref.at[0],
        left_ref.at[1],
        a_ref,
        b_ref,
        right_ref.at[0],
        right_ref.at[1],
    ]
    sides = (place_ref[1], 1 - place_ref[1])
    starts = [
        pl.multiple_of((lax.rem(place_ref[0] + 4 - s, 4) * 2 + side) * cols, cols)
        for s in range(4)
        for side in sides
    ]
    for first in range(0, width, 256):
        last = min(first + 256, width)
        weight = jnp.concatenate(
            [ref[first:last, pl.ds(start, cols)] for start in starts for ref in (gate_ref, up_ref)],
            axis=1,
        )
        for i in range(count):
            at = slice(i * size, (i + 1) * size)
            left = jnp.concatenate([ref[at, :] for ref in pieces], axis=1)
            out_refs[i][:, first:last] = contract_last(left, weight).astype(BF)


def input_parts(place, count, own, left, across_a, across_b, right, gate, up, *earlier):
    rows = own.shape[1]
    size = rows // count
    width, hidden = gate.shape
    arrays = (own, left, across_a, across_b, right, gate, up)
    return pl.pallas_call(
        lambda *refs: input_kernel(count, *refs),
        out_shape=[jax.ShapeDtypeStruct((size, width), BF)] * count,
        grid_spec=pltpu.PrefetchScalarGridSpec(
            num_scalar_prefetch=1,
            grid=(1,),
            in_specs=[whole(array.shape) for array in arrays]
            + [pl.BlockSpec(memory_space=pl.ANY)] * len(earlier),
            out_specs=[whole((size, width))] * count,
        ),
        compiler_params=pltpu.CompilerParams(vmem_limit_bytes=48 * 2**20),
        cost_estimate=pl.CostEstimate(
            flops=4 * rows * width * hidden,
            bytes_accessed=2 * rows * (width + 2 * hidden) + 4 * width * hidden,
            transcendentals=0,
        ),
    )(place, *arrays, *earlier)


def body(
    moe_grad,
    saved_act,
    route_prob,
    expert_ids,
    w_gate,
    w_up,
    w_down,
    queries,
    latent,
    rope_keys,
    w_ukv,
    latent_b,
    grad_kv_b,
):
    tokens, width = moe_grad.shape
    top_count = expert_ids.shape[1]
    share = saved_act.shape[3]
    xi, hi, zi, yi, ci = (lax.axis_index(name) for name in ("x", "h", "z", "y", "c"))
    experts = 32
    rows_y = 8 * QUEUE

    ukv_part = lax.dot_general(
        latent_b, grad_kv_b, (((0,), (0,)), ((), ())), preferred_element_type=F32
    ).astype(BF)
    hit = expert_ids[:, :, None] == jnp.arange(experts, dtype=jnp.int32)
    probs = jnp.sum(jnp.where(hit, route_prob[:, :, None].astype(F32), 0.0), axis=1)
    member_all = (probs > 0).astype(BF)
    spot_all = lax.dot_general(
        jnp.tril(jnp.ones((tokens, tokens), BF), -1),
        member_all,
        (((1,), (0,)), ((), ())),
        preferred_element_type=F32,
    )
    spot_own = jnp.sum(jnp.where(hit, spot_all[:, None, :], 0.0), axis=2).astype(jnp.int32)
    order = ((expert_ids // 2) % 4) * 8 + (expert_ids // 8) * 2 + expert_ids % 2
    target = (order * PADDED + spot_own).reshape(1, tokens * top_count)
    place = (target == jnp.arange(experts * PADDED, dtype=jnp.int32)[:, None]).astype(BF)
    send_saved = jnp.dot(
        place,
        saved_act.reshape(tokens * top_count, 2 * share),
        preferred_element_type=F32,
    ).astype(BF)

    near_a = (moe_grad, probs.T.astype(BF))
    far = [flip(array, "z", 2) for array in near_a]
    near_b = lax.optimization_barrier(
        tuple(jnp.stack(both) for both in zip(near_a, far)) + (send_saved, ukv_part)
    )
    near_b, send_saved, ukv_part = near_b[:2], near_b[2], near_b[3]
    near_c = [
        jnp.stack([pair[0], other[0], pair[1], other[1]])
        for pair, other in zip(near_b, [flip(array, "z", 1) for array in near_b])
    ]
    near_tokens, near_probs = lax.optimization_barrier(
        tuple(jnp.stack([array, flip(array, "c", 1)]) for array in near_c)
    )
    near_tokens = near_tokens.reshape(8 * tokens, width)
    got_saved = lax.all_to_all(
        send_saved, ("y", "z", "c"), split_axis=0, concat_axis=0, tiled=True
    ).reshape(4, 8 * PADDED, 2 * share)
    ukv_rows = ukv_part.shape[0] // 8
    ukv_all = lax.all_to_all(ukv_part, "x", split_axis=0, concat_axis=0, tiled=True)
    ukv_pair = jnp.sum(ukv_all.astype(F32).reshape(4, 2 * ukv_rows, ukv_part.shape[1]), axis=0)
    ukv_own = lax.dynamic_slice_in_dim(ukv_pair, hi * ukv_rows, ukv_rows, 0)
    ukv_far = lax.dynamic_slice_in_dim(ukv_pair, (1 - hi) * ukv_rows, ukv_rows, 0)
    ukv_grad = ukv_own + flip(ukv_far.astype(BF), "h", 1).astype(F32)

    picked = jnp.stack(
        [
            lax.dynamic_index_in_dim(near_probs, zi * 8 + ((yi + s) % 4) * 2 + ci, 2, False)
            for s in range(4)
        ]
    ).reshape(4, 8, tokens)
    member = picked > 0
    before = jnp.triu(jnp.ones((tokens, tokens), BF), 1)
    spot = lax.dot_general(
        member.astype(BF).reshape(32, tokens),
        before,
        (((1,), (0,)), ((), ())),
        preferred_element_type=F32,
    ).astype(jnp.int32)
    flips = jnp.arange(8, dtype=jnp.int32)
    block = ((flips % 4) ^ zi) * 2 + ((flips // 4) ^ ci)
    slot = spot.reshape(4, 8, tokens) + block[None, :, None] * QUEUE
    slot = jnp.where(member, slot, -1).reshape(4, 1, 8 * tokens)
    chosen = slot == jnp.arange(rows_y, dtype=jnp.int32)[None, :, None]
    picked = picked.reshape(4, 1, 8 * tokens)

    sent = [
        jnp.dot(
            jnp.where(chosen[s], picked[s], jnp.zeros((), BF)),
            near_tokens,
            preferred_element_type=F32,
        ).astype(BF)
        for s in range(4)
    ]
    arrived = [sent[0]] + [shift(sent[s], "y", s) for s in (1, 2, 3)]

    gate_factor, up_factor = factors(yi.astype(jnp.int32), got_saved, rows_y)
    here = jnp.stack([xi, hi]).astype(jnp.int32)
    first_parts = hidden_parts(
        xi, [arrived[s] for s in GROUPS[0]], w_down[0], arrived[2], got_saved
    )

    joined = jnp.concatenate(
        [latent, rope_keys, jnp.zeros((tokens, HD - ROPE), BF)], axis=1
    )
    joined = tie(joined, near_tokens)
    near_latents = lax.all_gather(joined, ("z", "y"), axis=0).reshape(4, 4, tokens, -1)
    far_latents = flip(near_latents, "c", 1)

    head_query = queries.reshape(queries.shape[0], 2, HD + ROPE).transpose(1, 2, 0)

    def attend(head):
        return attention(
            jnp.stack([xi * 2 + hi, zi, yi, ci]).astype(jnp.int32),
            head_query[head],
            near_latents,
            far_latents,
            w_ukv[:, 2 * HD * head : 2 * HD * (head + 1)],
        )

    returned = [None] * 4
    attn = [attend(0), attend(1)]
    for number, group in enumerate(GROUPS):
        if number:
            parts = hidden_parts(xi, [arrived[s] for s in group], w_down[0])
        else:
            parts = first_parts
        total = parts[0]
        for s in (1, 3, 2):
            total = total + shift(parts[s], "x", s).astype(F32)
        own_total = lax.dynamic_slice_in_dim(total, hi * share, share, 1)
        far_total = lax.dynamic_slice_in_dim(total, (1 - hi) * share, share, 1)
        hidden = own_total + flip(far_total.astype(BF), "h", 1).astype(F32)
        grads = jnp.concatenate(
            [
                (hidden * jnp.concatenate([array[s] for s in group], axis=0)).astype(BF)
                for array in (gate_factor, up_factor)
            ],
            axis=1,
        )
        pair = jnp.stack([grads, flip(grads, "h", 1)])
        left = shift(pair, "x", 1)
        right = shift(pair, "x", -1)
        across_a = shift(left[0], "x", 1)
        across_b = shift(right[1], "x", -1)
        ordered = (attn[0],) if number else (ukv_grad,)
        pieces = input_parts(
            here,
            len(group),
            pair,
            left,
            across_a,
            across_b,
            right,
            w_gate[0],
            w_up[0],
            *ordered,
        )
        for s, piece in zip(group, pieces):
            returned[s] = shift(piece, "y", -s) if s else piece

    gather_all = chosen.astype(BF)
    dense = sum(
        lax.dot_general(
            gather_all[s], returned[s], (((0,), (0,)), ((), ())), preferred_element_type=F32
        )
        for s in (0, 1, 3)
    )
    dense = (dense + combine(gather_all[2], returned[2], attn[1])).reshape(2, 4, tokens, width)
    sums = dense[0] + flip(dense[1].astype(BF), "c", 1).astype(F32)
    near_sums = flip(jnp.stack([sums[1], sums[3]]).astype(BF), "z", 1).astype(F32)
    first = sums[0] + near_sums[0]
    second = (sums[2] + near_sums[1]).astype(BF)
    moe_input_grad = (first + flip(second, "z", 2).astype(F32)).astype(BF)
    attn_out = jnp.concatenate(attn, axis=1)
    return (moe_input_grad, attn_out, ukv_grad)


def solution(mesh):
    fine = Mesh(mesh.devices.reshape(4, 2, 4, 4, 2), ("x", "h", "z", "y", "c"))
    dp = ("x", "h")
    expert = ("z", "y", "c")
    in_specs = (
        P(expert, dp),
        P(expert, None, None, dp),
        P(expert, None),
        P(expert, None),
        P(expert, dp, None),
        P(expert, dp, None),
        P(expert, None, dp),
        P(dp, expert),
        P(expert, None),
        P(expert, None),
        P(None, expert),
        P(dp, None),
        P(dp, expert),
    )
    out_specs = (P(expert, dp), P(dp, expert), P(dp, expert))
    return jax.shard_map(body, mesh=fine, in_specs=in_specs, out_specs=out_specs, check_vma=False)
```

```python
import jax
import jax.numpy as jnp
from jax import lax
from jax.experimental import pallas as pl
from jax.experimental.pallas import tpu as pltpu
from jax.sharding import Mesh
from jax.sharding import PartitionSpec as P

HD = 128
ROPE = 64
QUEUE = 42
PADDED = 48
GROUPS = ((1, 3), (2, 0))
LOG2E = 1.4426950408889634
BF = jnp.bfloat16
F32 = jnp.float32


def contract_last(left, right):
    return lax.dot_general(left, right, (((1,), (1,)), ((), ())), preferred_element_type=F32)


def flip(array, axis, bit):
    size = lax.axis_size(axis)
    return lax.ppermute(array, axis, [(i, i ^ bit) for i in range(size)])


def shift(array, axis, step):
    size = lax.axis_size(axis)
    return lax.ppermute(array, axis, [(i, (i + step) % size) for i in range(size)])


def tie(value, *others):
    return lax.optimization_barrier((value, *others))[0]


def whole(shape):
    return pl.BlockSpec(shape, lambda *_: (0,) * len(shape))


def attention_kernel(place_ref, query_ref, *refs):
    latent_refs, (weight_ref, out_ref, top, total, acc) = refs[:4], refs[4:]
    step = pl.program_id(0)
    own = place_ref[0]
    rows = query_ref.shape[1]
    size = latent_refs[0].shape[2]
    keys = 4 * size
    tile = min(256, rows)
    factor = (HD + ROPE) ** (-0.5) * LOG2E

    @pl.when(step == 0)
    def _():
        top[...] = jnp.full(top.shape, -1e30, F32)
        total[...] = jnp.zeros(total.shape, F32)
        acc[...] = jnp.zeros(acc.shape, F32)

    def work(masked):
        joined = jnp.concatenate([ref[0, 0] for ref in latent_refs], axis=0)
        both = jnp.dot(joined[:, : 4 * HD], weight_ref[...], preferred_element_type=F32)
        key = jnp.concatenate(
            [both[:, :HD].astype(BF), joined[:, 4 * HD : 4 * HD + ROPE]], axis=1
        )
        value = both[:, HD:].T.astype(BF)
        for part in range(rows // tile):
            at = slice(part * tile, (part + 1) * tile)
            scores = jnp.dot(key, query_ref[:, at], preferred_element_type=F32)
            if masked:
                line = lax.broadcasted_iota(jnp.int32, (size, tile), 0)
                row = jnp.concatenate(
                    [
                        line + (pair * 2 * size + (place_ref[3] ^ flipped) * size)
                        for pair in range(2)
                        for flipped in range(2)
                    ],
                    axis=0,
                )
                col = lax.broadcasted_iota(jnp.int32, (keys, tile), 1) + part * tile
                scores = jnp.where(row <= col, scores, -1e30)
            before = top[:, at]
            now = jnp.maximum(before, jnp.max(scores, axis=0, keepdims=True))
            scale = jnp.exp2((before - now) * factor)
            expo = jnp.exp2((scores - now) * factor)
            total[:, at] = total[:, at] * scale + jnp.sum(expo, axis=0, keepdims=True)
            acc[:, at] = acc[:, at] * scale + jnp.dot(
                value, expo.astype(BF), preferred_element_type=F32
            )
            top[:, at] = now

    @pl.when(step < own)
    def _():
        work(False)

    @pl.when(step == own)
    def _():
        work(True)

    @pl.when(step == pl.num_programs(0) - 1)
    def _():
        out_ref[...] = (acc[...] / total[...]).T.astype(BF)


def attention(place, head_query, near_latents, far_latents, weight):
    width, rows = head_query.shape
    _, _, size, depth = near_latents.shape
    steps = 8

    def latent_spec(pair):
        def index(j, place):
            step = jnp.minimum(j, place[0])
            return (lax.div(step, 2), lax.rem(step, 2) * 2 + pair, 0, 0)

        return pl.BlockSpec((1, 1, size, depth), index)

    return pl.pallas_call(
        attention_kernel,
        out_shape=jax.ShapeDtypeStruct((rows, HD), BF),
        grid_spec=pltpu.PrefetchScalarGridSpec(
            num_scalar_prefetch=1,
            grid=(steps,),
            in_specs=[
                whole((width, rows)),
                latent_spec(0),
                latent_spec(0),
                latent_spec(1),
                latent_spec(1),
                whole(weight.shape),
            ],
            out_specs=whole((rows, HD)),
            scratch_shapes=[
                pltpu.VMEM((1, rows), F32),
                pltpu.VMEM((1, rows), F32),
                pltpu.VMEM((HD, rows), F32),
            ],
        ),
        compiler_params=pltpu.CompilerParams(vmem_limit_bytes=32 * 2**20),
        cost_estimate=pl.CostEstimate(
            flops=2 * steps * rows * (rows * 320 + 512 * 256),
            bytes_accessed=2 * steps * rows * depth,
            transcendentals=steps * rows * rows,
        ),
    )(
        place,
        head_query,
        near_latents,
        far_latents,
        near_latents,
        far_latents,
        weight,
    )


def hidden_kernel(count, place_ref, *refs):
    rows_refs, weight_ref, out_refs = refs[:count], refs[count], refs[-4:]
    size = rows_refs[0].shape[0]
    cols = out_refs[0].shape[1]
    for s in range(4):
        at = pl.multiple_of(lax.rem(place_ref[0] + s, 4) * cols, cols)
        weight = weight_ref[pl.ds(at, cols), :]
        for i in range(count):
            out_refs[s][i * size : (i + 1) * size, :] = contract_last(
                rows_refs[i][...], weight
            ).astype(out_refs[s].dtype)


def hidden_parts(place, rows, weight, *earlier):
    count = len(rows)
    size, width = rows[0].shape
    hidden = weight.shape[0]
    shape = (count * size, hidden // 4)
    kinds = [F32, BF, BF, BF]
    return pl.pallas_call(
        lambda *refs: hidden_kernel(count, *refs),
        out_shape=[jax.ShapeDtypeStruct(shape, kind) for kind in kinds],
        grid_spec=pltpu.PrefetchScalarGridSpec(
            num_scalar_prefetch=1,
            grid=(1,),
            in_specs=[whole((size, width))] * count
            + [whole(weight.shape)]
            + [pl.BlockSpec(memory_space=pl.ANY)] * len(earlier),
            out_specs=[whole(shape)] * 4,
        ),
        compiler_params=pltpu.CompilerParams(vmem_limit_bytes=32 * 2**20),
        cost_estimate=pl.CostEstimate(
            flops=2 * count * size * width * hidden,
            bytes_accessed=2 * count * size * (width + hidden) + 2 * width * hidden,
            transcendentals=0,
        ),
    )(place.reshape(1), *rows, weight, *earlier)


def factor_kernel(place_ref, saved_ref, gate_ref, up_ref):
    rows = gate_ref.shape[1]
    share = saved_ref.shape[2] // 2
    slot = lax.broadcasted_iota(jnp.int32, (rows, saved_ref.shape[1]), 0)
    spot = lax.broadcasted_iota(jnp.int32, (rows, saved_ref.shape[1]), 1)
    block = lax.div(slot, QUEUE)
    keep = (block * PADDED + (slot - block * QUEUE) == spot).astype(BF)
    for s in range(4):
        source = lax.rem(place_ref[0] + 4 - s, 4)
        saved = jnp.dot(keep, saved_ref[source], preferred_element_type=F32)
        gate_pre, up_pre = saved[:, :share], saved[:, share:]
        sigmoid_gate = 1.0 / (1.0 + jnp.exp(-gate_pre))
        gate_ref[s] = up_pre * sigmoid_gate * (1.0 + gate_pre * (1.0 - sigmoid_gate))
        up_ref[s] = gate_pre * sigmoid_gate


def factors(place, saved, rows):
    shape = (4, rows, saved.shape[2] // 2)
    return pl.pallas_call(
        factor_kernel,
        out_shape=[jax.ShapeDtypeStruct(shape, F32)] * 2,
        grid_spec=pltpu.PrefetchScalarGridSpec(
            num_scalar_prefetch=1,
            grid=(1,),
            in_specs=[whole(saved.shape)],
            out_specs=[whole(shape)] * 2,
        ),
        compiler_params=pltpu.CompilerParams(vmem_limit_bytes=24 * 2**20),
        cost_estimate=pl.CostEstimate(
            flops=8 * rows * saved.shape[1] * saved.shape[2],
            bytes_accessed=2 * saved.size + 32 * rows * shape[2],
            transcendentals=4 * rows * shape[2],
        ),
    )(place.reshape(1), saved)


def combine_kernel(chosen_ref, rows_ref, *refs):
    refs[-1][...] = lax.dot_general(
        chosen_ref[...], rows_ref[...], (((0,), (0,)), ((), ())), preferred_element_type=F32
    )


def combine(chosen, rows, *earlier):
    shape = (chosen.shape[1], rows.shape[1])
    return pl.pallas_call(
        combine_kernel,
        out_shape=jax.ShapeDtypeStruct(shape, F32),
        grid=(1,),
        in_specs=[whole(chosen.shape), whole(rows.shape)]
        + [pl.BlockSpec(memory_space=pl.ANY)] * len(earlier),
        out_specs=whole(shape),
        compiler_params=pltpu.CompilerParams(vmem_limit_bytes=24 * 2**20),
        cost_estimate=pl.CostEstimate(
            flops=2 * shape[0] * rows.size,
            bytes_accessed=2 * (chosen.size + rows.size) + 4 * shape[0] * shape[1],
            transcendentals=0,
        ),
    )(chosen, rows, *earlier)


def input_kernel(
    count, place_ref, own_ref, left_ref, a_ref, b_ref, right_ref, gate_ref, up_ref, *rest
):
    out_refs = rest[-count:]
    size = out_refs[0].shape[0]
    cols = own_ref.shape[2] // 2
    width = gate_ref.shape[0]
    pieces = [
        own_ref.at[0],
        own_ref.at[1],
        left_ref.at[0],
        left_ref.at[1],
        a_ref,
        b_ref,
        right_ref.at[0],
        right_ref.at[1],
    ]
    sides = (place_ref[1], 1 - place_ref[1])
    starts = [
        pl.multiple_of((lax.rem(place_ref[0] + 4 - s, 4) * 2 + side) * cols, cols)
        for s in range(4)
        for side in sides
    ]
    for first in range(0, width, 256):
        last = min(first + 256, width)
        weight = jnp.concatenate(
            [ref[first:last, pl.ds(start, cols)] for start in starts for ref in (gate_ref, up_ref)],
            axis=1,
        )
        for i in range(count):
            at = slice(i * size, (i + 1) * size)
            left = jnp.concatenate([ref[at, :] for ref in pieces], axis=1)
            out_refs[i][:, first:last] = contract_last(left, weight).astype(BF)


def input_parts(place, count, own, left, across_a, across_b, right, gate, up, *earlier):
    rows = own.shape[1]
    size = rows // count
    width, hidden = gate.shape
    arrays = (own, left, across_a, across_b, right, gate, up)
    return pl.pallas_call(
        lambda *refs: input_kernel(count, *refs),
        out_shape=[jax.ShapeDtypeStruct((size, width), BF)] * count,
        grid_spec=pltpu.PrefetchScalarGridSpec(
            num_scalar_prefetch=1,
            grid=(1,),
            in_specs=[whole(array.shape) for array in arrays]
            + [pl.BlockSpec(memory_space=pl.ANY)] * len(earlier),
            out_specs=[whole((size, width))] * count,
        ),
        compiler_params=pltpu.CompilerParams(vmem_limit_bytes=48 * 2**20),
        cost_estimate=pl.CostEstimate(
            flops=4 * rows * width * hidden,
            bytes_accessed=2 * rows * (width + 2 * hidden) + 4 * width * hidden,
            transcendentals=0,
        ),
    )(place, *arrays, *earlier)


def body(
    moe_grad,
    saved_act,
    route_prob,
    expert_ids,
    w_gate,
    w_up,
    w_down,
    queries,
    latent,
    rope_keys,
    w_ukv,
    latent_b,
    grad_kv_b,
):
    tokens, width = moe_grad.shape
    top_count = expert_ids.shape[1]
    share = saved_act.shape[3]
    xi, hi, zi, yi, ci = (lax.axis_index(name) for name in ("x", "h", "z", "y", "c"))
    experts = 32
    rows_y = 8 * QUEUE

    ukv_part = lax.dot_general(
        latent_b, grad_kv_b, (((0,), (0,)), ((), ())), preferred_element_type=F32
    ).astype(BF)
    hit = expert_ids[:, :, None] == jnp.arange(experts, dtype=jnp.int32)
    probs = jnp.sum(jnp.where(hit, route_prob[:, :, None].astype(F32), 0.0), axis=1)
    member_all = (probs > 0).astype(BF)
    spot_all = lax.dot_general(
        jnp.tril(jnp.ones((tokens, tokens), BF), -1),
        member_all,
        (((1,), (0,)), ((), ())),
        preferred_element_type=F32,
    )
    spot_own = jnp.sum(jnp.where(hit, spot_all[:, None, :], 0.0), axis=2).astype(jnp.int32)
    order = ((expert_ids // 2) % 4) * 8 + (expert_ids // 8) * 2 + expert_ids % 2
    target = (order * PADDED + spot_own).reshape(1, tokens * top_count)
    place = (target == jnp.arange(experts * PADDED, dtype=jnp.int32)[:, None]).astype(BF)
    send_saved = jnp.dot(
        place,
        saved_act.reshape(tokens * top_count, 2 * share),
        preferred_element_type=F32,
    ).astype(BF)

    near_a = (moe_grad, probs.T.astype(BF))
    far = [flip(array, "z", 2) for array in near_a]
    near_b = lax.optimization_barrier(
        tuple(jnp.stack(both) for both in zip(near_a, far)) + (send_saved, ukv_part)
    )
    near_b, send_saved, ukv_part = near_b[:2], near_b[2], near_b[3]
    near_c = [
        jnp.stack([pair[0], other[0], pair[1], other[1]])
        for pair, other in zip(near_b, [flip(array, "z", 1) for array in near_b])
    ]
    near_tokens, near_probs = lax.optimization_barrier(
        tuple(jnp.stack([array, flip(array, "c", 1)]) for array in near_c)
    )
    near_tokens = near_tokens.reshape(8 * tokens, width)
    got_saved = lax.all_to_all(
        send_saved, ("y", "z", "c"), split_axis=0, concat_axis=0, tiled=True
    ).reshape(4, 8 * PADDED, 2 * share)
    ukv_rows = ukv_part.shape[0] // 8
    ukv_all = lax.all_to_all(ukv_part, "x", split_axis=0, concat_axis=0, tiled=True)
    ukv_pair = jnp.sum(ukv_all.astype(F32).reshape(4, 2 * ukv_rows, ukv_part.shape[1]), axis=0)
    ukv_own = lax.dynamic_slice_in_dim(ukv_pair, hi * ukv_rows, ukv_rows, 0)
    ukv_far = lax.dynamic_slice_in_dim(ukv_pair, (1 - hi) * ukv_rows, ukv_rows, 0)
    ukv_grad = ukv_own + flip(ukv_far.astype(BF), "h", 1).astype(F32)

    picked = jnp.stack(
        [
            lax.dynamic_index_in_dim(near_probs, zi * 8 + ((yi + s) % 4) * 2 + ci, 2, False)
            for s in range(4)
        ]
    ).reshape(4, 8, tokens)
    member = picked > 0
    before = jnp.triu(jnp.ones((tokens, tokens), BF), 1)
    spot = lax.dot_general(
        member.astype(BF).reshape(32, tokens),
        before,
        (((1,), (0,)), ((), ())),
        preferred_element_type=F32,
    ).astype(jnp.int32)
    flips = jnp.arange(8, dtype=jnp.int32)
    block = ((flips % 4) ^ zi) * 2 + ((flips // 4) ^ ci)
    slot = spot.reshape(4, 8, tokens) + block[None, :, None] * QUEUE
    slot = jnp.where(member, slot, -1).reshape(4, 1, 8 * tokens)
    chosen = slot == jnp.arange(rows_y, dtype=jnp.int32)[None, :, None]
    picked = picked.reshape(4, 1, 8 * tokens)

    sent = [
        jnp.dot(
            jnp.where(chosen[s], picked[s], jnp.zeros((), BF)),
            near_tokens,
            preferred_element_type=F32,
        ).astype(BF)
        for s in range(4)
    ]
    arrived = [sent[0]] + [shift(sent[s], "y", s) for s in (1, 2, 3)]

    gate_factor, up_factor = factors(yi.astype(jnp.int32), got_saved, rows_y)
    here = jnp.stack([xi, hi]).astype(jnp.int32)
    first_parts = hidden_parts(
        xi, [arrived[s] for s in GROUPS[0]], w_down[0], arrived[2], got_saved, ukv_grad
    )

    joined = jnp.concatenate(
        [latent, rope_keys, jnp.zeros((tokens, HD - ROPE), BF)], axis=1
    )
    joined = tie(joined, near_tokens)
    near_latents = lax.all_gather(joined, ("z", "y"), axis=0).reshape(4, 4, tokens, -1)
    far_latents = flip(near_latents, "c", 1)

    head_query = queries.reshape(queries.shape[0], 2, HD + ROPE).transpose(1, 2, 0)

    def attend(head):
        return attention(
            jnp.stack([xi * 2 + hi, zi, yi, ci]).astype(jnp.int32),
            head_query[head],
            near_latents,
            far_latents,
            w_ukv[:, 2 * HD * head : 2 * HD * (head + 1)],
        )

    returned = [None] * 4
    attn = [attend(0), attend(1)]
    for number, group in enumerate(GROUPS):
        if number:
            parts = hidden_parts(xi, [arrived[s] for s in group], w_down[0])
        else:
            parts = first_parts
        total = parts[0]
        for s in (1, 3, 2):
            total = total + shift(parts[s], "x", s).astype(F32)
        own_total = lax.dynamic_slice_in_dim(total, hi * share, share, 1)
        far_total = lax.dynamic_slice_in_dim(total, (1 - hi) * share, share, 1)
        hidden = own_total + flip(far_total.astype(BF), "h", 1).astype(F32)
        grads = jnp.concatenate(
            [
                (hidden * jnp.concatenate([array[s] for s in group], axis=0)).astype(BF)
                for array in (gate_factor, up_factor)
            ],
            axis=1,
        )
        pair = jnp.stack([grads, flip(grads, "h", 1)])
        left = shift(pair, "x", 1)
        right = shift(pair, "x", -1)
        across_a = shift(left[0], "x", 1)
        across_b = shift(right[1], "x", -1)
        ordered = (attn[0],) if number else ()
        pieces = input_parts(
            here,
            len(group),
            pair,
            left,
            across_a,
            across_b,
            right,
            w_gate[0],
            w_up[0],
            *ordered,
        )
        for s, piece in zip(group, pieces):
            returned[s] = shift(piece, "y", -s) if s else piece

    gather_all = chosen.astype(BF)
    dense = sum(
        lax.dot_general(
            gather_all[s], returned[s], (((0,), (0,)), ((), ())), preferred_element_type=F32
        )
        for s in (0, 1, 3)
    )
    dense = (dense + combine(gather_all[2], returned[2], attn[1])).reshape(2, 4, tokens, width)
    sums = dense[0] + flip(dense[1].astype(BF), "c", 1).astype(F32)
    near_sums = flip(jnp.stack([sums[1], sums[3]]).astype(BF), "z", 1).astype(F32)
    first = sums[0] + near_sums[0]
    second = (sums[2] + near_sums[1]).astype(BF)
    moe_input_grad = (first + flip(second, "z", 2).astype(F32)).astype(BF)
    attn_out = jnp.concatenate(attn, axis=1)
    return (moe_input_grad, attn_out, ukv_grad)


def solution(mesh):
    fine = Mesh(mesh.devices.reshape(4, 2, 4, 4, 2), ("x", "h", "z", "y", "c"))
    dp = ("x", "h")
    expert = ("z", "y", "c")
    in_specs = (
        P(expert, dp),
        P(expert, None, None, dp),
        P(expert, None),
        P(expert, None),
        P(expert, dp, None),
        P(expert, dp, None),
        P(expert, None, dp),
        P(dp, expert),
        P(expert, None),
        P(expert, None),
        P(None, expert),
        P(dp, None),
        P(dp, expert),
    )
    out_specs = (P(expert, dp), P(dp, expert), P(dp, expert))
    return jax.shard_map(body, mesh=fine, in_specs=in_specs, out_specs=out_specs, check_vma=False)
```
